256 devices in a mesh: outer: 8 (over z), inner: 32 (over x, y, core).
Axes of the slice: x: 4, y: 4, z: 8, core: 2. Of those that a mesh axis runs over, the one named last changes fastest.
Arguments:
- query: bfloat16 [32768, 16, 128], P(('outer', 'inner')), may hold values from -6 to 6
- key_inputs: bfloat16 [32768, 16, 128], P(('outer', 'inner')), may hold values from -6 to 6
- value_inputs: bfloat16 [32768, 16, 128], P(('outer', 'inner')), may hold values from -6 to 6
- output_gradient: bfloat16 [32768, 16, 128], P(('outer', 'inner')), may hold values from -6 to 6
Outputs:
- grad_query: bfloat16 [32768, 16, 128], P(('outer', 'inner'))
- grad_key: bfloat16 [32768, 16, 128], P(('outer', 'inner'))
- grad_value: bfloat16 [32768, 16, 128], P(('outer', 'inner'))
The draws below stay inside these ranges and needn't reach their ends.
All inputs are finite; a program needn't handle non-finite values.
Results may differ from the reference program's by a relative error of at most 0.005.
Values sent between devices are 32-bit elements; how exact they have to be, the bound alone decides.
A program may use at most 192 MiB of HBM per device.

```python
import jax
import jax.numpy as jnp
from jax import lax

HEADS = 16
DK = 128
TOK_DEV = 128
TOKENS = 32768


def levels(stream_key, extent, pieces, least, largest):
    factor_of, own = 1.0, jax.random.fold_in(stream_key, 6)
    for axis_at, shards_of in pieces:
        heights = jnp.exp(jax.random.uniform(jax.random.fold_in(own, axis_at), (shards_of,), jnp.float32, least / len(pieces), largest / len(pieces)))
        factor_of = factor_of * jnp.repeat(heights, extent[axis_at] // shards_of).reshape([-1 if axis == axis_at else 1 for axis in range(len(extent))])
    return factor_of


def gaussian(own_key, shape, deviation, limit, shards=(), dtype=jnp.bfloat16):
    entries = deviation * jax.random.normal(own_key, shape, jnp.float32)
    if shards:
        entries = entries * levels(own_key, shape, shards, -0.22, 0.18)
    return jnp.clip(entries, -limit, limit).astype(dtype)


def setup_inputs(seed: int = 0) -> dict:
    key_list = jax.random.split(jax.random.key(seed), 5)
    query = gaussian(key_list[0], (TOKENS, HEADS, DK), 1.0, 6.0, ((0, 256),))
    key_inputs = gaussian(key_list[1], (TOKENS, HEADS, DK), 1.0, 6.0, ((0, 256),))
    value_inputs = gaussian(key_list[2], (TOKENS, HEADS, DK), 1.0, 6.0, ((0, 256),))
    output_gradient = gaussian(key_list[3], (TOKENS, HEADS, DK), 1.0, 6.0, ((0, 256),))
    return dict(query=query, key_inputs=key_inputs, value_inputs=value_inputs, output_gradient=output_gradient)


def lower_triangle(x):
    return lax.optimization_barrier(x.astype(jnp.bfloat16)).astype(jnp.float32)


def reference(query, key_inputs, value_inputs, output_gradient):
    blocks = TOKENS // TOK_DEV
    scale = (DK * TOKENS) ** -0.5
    shape = (blocks, TOK_DEV, HEADS, DK)
    qry = query.reshape(shape)
    kys = key_inputs.reshape(shape)
    vls = value_inputs.reshape(shape)
    dos = output_gradient.reshape(shape)
    rows = lax.broadcasted_iota(jnp.int32, (TOK_DEV, TOK_DEV), 0)
    cols = lax.broadcasted_iota(jnp.int32, (TOK_DEV, TOK_DEV), 1)
    causal = (cols <= rows)[None]

    def masked(a, b):
        full = jnp.einsum('thk,shk->hts', a.astype(jnp.float32), b.astype(jnp.float32))
        return lower_triangle(jnp.where(causal, full, jnp.float32(0.0)))

    def forward(prefix_running, items):
        query_matrix, key_matrix, value_matrix, feature_width = items
        dprob = masked(feature_width, value_matrix)
        inner_part = jnp.einsum('hts,shk->thk', dprob, key_matrix.astype(jnp.float32))
        outer_portion = jnp.einsum('swx,wmx->swm', feature_width.astype(jnp.float32), lower_triangle(prefix_running))
        grad_q = (scale * (inner_part + outer_portion)).astype(jnp.bfloat16)
        running_state = jnp.einsum('xfw,xfs->fws', key_matrix.astype(jnp.float32), value_matrix.astype(jnp.float32))
        return prefix_running + running_state, grad_q

    def backward(suffix, items):
        query_matrix, key_matrix, value_matrix, feature_width = items
        dprob = masked(feature_width, value_matrix)
        score = masked(query_matrix, key_matrix)
        suffix_lower = lower_triangle(suffix)
        key_gradient = jnp.einsum('hts,thk->shk', dprob, query_matrix.astype(jnp.float32))
        key_gradient = key_gradient + jnp.einsum('ujt,jit->uji', value_matrix.astype(jnp.float32), suffix_lower)
        value_gradient = jnp.einsum('hts,thv->shv', score, feature_width.astype(jnp.float32))
        value_gradient = value_gradient + jnp.einsum('diw,iwf->dif', key_matrix.astype(jnp.float32), suffix_lower)
        running_state = jnp.einsum('xfw,xfs->fws', query_matrix.astype(jnp.float32), feature_width.astype(jnp.float32))
        return suffix + running_state, ((scale * key_gradient).astype(jnp.bfloat16), (scale * value_gradient).astype(jnp.bfloat16))

    zeros = jnp.zeros((HEADS, DK, DK), jnp.float32)
    unused, grad_query = lax.scan(forward, zeros, (qry, kys, vls, dos))
    unused2, grads = lax.scan(backward, zeros, (qry, kys, vls, dos), reverse=True)
    full = (TOKENS, HEADS, DK)
    return grad_query.reshape(full), grads[0].reshape(full), grads[1].reshape(full)
```

```python
import functools

import jax
import jax.numpy as jnp
from jax import lax
from jax.experimental import pallas as pl
from jax.experimental.pallas import tpu as pltpu
from jax.sharding import PartitionSpec as P

MESH = pl.DeviceIdType.MESH
GROUPS = 2

PAIR, UP, ALONG, DOWN, BACK = range(5)


def nn(a, b):
    return lax.dot_general(a, b, (((1,), (0,)), ((), ())), preferred_element_type=jnp.float32)


def nt(a, b):
    return lax.dot_general(a, b, (((1,), (1,)), ((), ())), preferred_element_type=jnp.float32)


def tn(a, b):
    return lax.dot_general(a, b, (((0,), (0,)), ((), ())), preferred_element_type=jnp.float32)


def kernel(
    dims, scale,
    q_ref, k_ref, v_ref, g_ref, dq_ref, dk_ref, dv_ref,
    qt, kt, vt, gt, acc, res, own, pair, chip, got, plane, along, down, base, back, final,
    send, recv,
):
    nz, nxy, groups = dims
    heads, tok, dim = qt.shape
    per = heads // groups
    half = per // 2
    rows = half * dim
    r = rows // nxy
    z = lax.axis_index("outer")
    inner = lax.axis_index("inner")
    xy, core = inner // 2, inner % 2

    def there(dz, dxy, dcore):
        return (lax.rem(z + dz, nz), lax.rem(xy + dxy, nxy) * 2 + lax.rem(core + dcore, 2))

    partners = [there(0, 0, 1)]
    partners += [there(0, k, 0) for k in range(1, nxy)]
    partners += [there(k, 0, 0) for k in range(1, nz)]
    barrier = pltpu.get_barrier_semaphore()
    for who in partners:
        pl.semaphore_signal(barrier, inc=1, device_id=who, device_id_type=MESH)

    def remote(src, dst, stage, g, who):
        return pltpu.make_async_remote_copy(
            src_ref=src, dst_ref=dst, send_sem=send.at[stage, g], recv_sem=recv.at[stage, g],
            device_id=who, device_id_type=MESH,
        )

    def arrived(ref, stage, g):
        pltpu.make_async_copy(ref, ref, recv.at[stage, g]).wait()

    def left(ref, stage, g):
        pltpu.make_async_copy(ref, ref, send.at[stage, g]).wait()

    kt[...] = jnp.swapaxes(k_ref[...], 0, 1)
    vt[...] = jnp.swapaxes(v_ref[...], 0, 1)
    qt[...] = jnp.swapaxes(q_ref[...], 0, 1)
    gt[...] = jnp.swapaxes(g_ref[...], 0, 1)

    def states(g):
        for part in range(2):
            def one(j, _, part=part):
                h = g * per + part * half + j
                at = pl.ds(pl.multiple_of(j * dim, dim), dim)
                own[g, part, 0, at] = tn(kt[h], vt[h])
                own[g, part, 1, at] = tn(qt[h], gt[h])
                return 0
            lax.fori_loop(0, half, one, 0, unroll=2)

    def pair_start(g):
        remote(own.at[g, 1 - core], pair.at[g], PAIR, g, there(0, 0, 1)).start()

    def up_start(g):
        arrived(pair.at[g], PAIR, g)
        for s in range(2):
            total = own[g, core, s] + pair[g, s]
            chip[g, :, s] = total.reshape(nxy, r, dim)
        pltpu.make_async_copy(chip.at[g, xy], got.at[g, xy], recv.at[UP, g]).start()
        for k in range(1, nxy):
            who = lax.rem(xy + k, nxy)
            remote(chip.at[g, who], got.at[g, xy], UP, g, there(0, k, 0)).start()

    def along_start(g):
        arrived(got.at[g], UP, g)
        plane[g] = jnp.sum(got[g], axis=0)
        for k in range(1, nz):
            later = lax.rem(z + k, nz) > z
            remote(plane.at[g, jnp.where(later, 0, 1)], along.at[g, k - 1], ALONG, g, there(k, 0, 0)).start()

    def down_start(g):
        arrived(along.at[g], ALONG, g)
        before = jnp.zeros((r, dim), jnp.float32)
        after = jnp.zeros((r, dim), jnp.float32)
        for k in range(1, nz):
            value = along[g, k - 1]
            before = before + jnp.where(k <= z, value, 0.0)
            after = after + jnp.where(k > z, value, 0.0)
        for i in range(nxy):
            down[g, i, 0] = before
            before = before + got[g, i, 0]
        for i in reversed(range(nxy)):
            down[g, i, 1] = after
            after = after + got[g, i, 1]
        pltpu.make_async_copy(down.at[g, xy], base.at[g, xy], recv.at[DOWN, g]).start()
        for k in range(1, nxy):
            who = lax.rem(xy + k, nxy)
            remote(down.at[g, who], base.at[g, xy], DOWN, g, there(0, k, 0)).start()

    def back_start(g):
        arrived(base.at[g], DOWN, g)
        first = core == 0
        before = base[g, :, 0].reshape(rows, dim)
        after = base[g, :, 1].reshape(rows, dim)
        back[g, 0] = before + jnp.where(first, own[g, core, 0], 0.0)
        back[g, 1] = after + jnp.where(first, 0.0, own[g, core, 1])
        remote(back.at[g], final.at[g, 1], BACK, g, there(0, 0, 1)).start()
        final[g, 0, 0] = before + jnp.where(first, 0.0, pair[g, 0])
        final[g, 0, 1] = after + jnp.where(first, pair[g, 1], 0.0)

    def local(h, _):
        at = lax.broadcasted_iota(jnp.int32, (tok, tok), 0)
        to = lax.broadcasted_iota(jnp.int32, (tok, tok), 1)
        q, k, v, d = qt[h], kt[h], vt[h], gt[h]
        dprob = jnp.where(to <= at, nt(d, v), 0.0).astype(jnp.bfloat16)
        dprob_t = jnp.where(at <= to, nt(v, d), 0.0).astype(jnp.bfloat16)
        score_t = jnp.where(at <= to, nt(k, q), 0.0).astype(jnp.bfloat16)
        acc[0, h] = nn(dprob, k)
        acc[1, h] = nn(dprob_t, q)
        acc[2, h] = nn(score_t, d)
        return 0

    def finish(g, which):
        part = core if which == 0 else 1 - core

        def one(j, _):
            h = g * per + part * half + j
            at = pl.ds(pl.multiple_of(j * dim, dim), dim)
            before = final[g, which, 0, at].astype(jnp.bfloat16)
            after = final[g, which, 1, at].astype(jnp.bfloat16)
            res[0, h] = (scale * (acc[0, h] + nt(gt[h], before))).astype(jnp.bfloat16)
            res[1, h] = (scale * (acc[1, h] + nt(vt[h], after))).astype(jnp.bfloat16)
            res[2, h] = (scale * (acc[2, h] + nn(kt[h], after))).astype(jnp.bfloat16)
            return 0

        lax.fori_loop(0, half, one, 0, unroll=2)

    def local_group(g):
        lax.fori_loop(g * per, (g + 1) * per, local, 0, unroll=2)

    states(0)
    pl.semaphore_wait(barrier, len(partners))
    pair_start(0)
    for g in range(1, groups):
        states(g)
        pair_start(g)
        up_start(g - 1)
    up_start(groups - 1)
    for g in range(groups):
        local_group(g)
    for g in range(groups):
        along_start(g)
        if g >= 1:
            down_start(g - 1)
    down_start(groups - 1)
    for g in range(groups):
        back_start(g)
        finish(g, 0)
        arrived(final.at[g, 1], BACK, g)
        finish(g, 1)
    dq_ref[...] = jnp.swapaxes(res[0], 0, 1)
    dk_ref[...] = jnp.swapaxes(res[1], 0, 1)
    dv_ref[...] = jnp.swapaxes(res[2], 0, 1)

    for g in range(groups):
        left(pair.at[g], PAIR, g)
        left(chip.at[g, pl.ds(0, nxy - 1)], UP, g)
        left(along.at[g], ALONG, g)
        left(down.at[g, pl.ds(0, nxy - 1)], DOWN, g)
        left(back.at[g], BACK, g)


def solution(mesh):
    nz, nxy = mesh.shape["outer"], mesh.shape["inner"] // 2
    groups = GROUPS

    def step(q, k, v, g):
        tok, heads, dim = q.shape
        scale = (dim * tok * mesh.size) ** -0.5
        rows = heads // groups // 2 * dim
        r = rows // nxy
        f32, low = jnp.float32, jnp.bfloat16
        vmem = pl.BlockSpec(memory_space=pltpu.VMEM)
        return pl.pallas_call(
            functools.partial(kernel, (nz, nxy, groups), scale),
            out_shape=[jax.ShapeDtypeStruct((tok, heads, dim), low)] * 3,
            in_specs=[vmem] * 4,
            out_specs=[vmem] * 3,
            scratch_shapes=[
                pltpu.VMEM((heads, tok, dim), low),
                pltpu.VMEM((heads, tok, dim), low),
                pltpu.VMEM((heads, tok, dim), low),
                pltpu.VMEM((heads, tok, dim), low),
                pltpu.VMEM((3, heads, tok, dim), f32),
                pltpu.VMEM((3, heads, tok, dim), low),
                pltpu.VMEM((groups, 2, 2, rows, dim), f32),
                pltpu.VMEM((groups, 2, rows, dim), f32),
                pltpu.VMEM((groups, nxy, 2, r, dim), f32),
                pltpu.VMEM((groups, nxy, 2, r, dim), f32),
                pltpu.VMEM((groups, 2, r, dim), f32),
                pltpu.VMEM((groups, nz - 1, r, dim), f32),
                pltpu.VMEM((groups, nxy, 2, r, dim), f32),
                pltpu.VMEM((groups, nxy, 2, r, dim), f32),
                pltpu.VMEM((groups, 2, rows, dim), f32),
                pltpu.VMEM((groups, 2, 2, rows, dim), f32),
                pltpu.SemaphoreType.DMA((5, groups)),
                pltpu.SemaphoreType.DMA((5, groups)),
            ],
            compiler_params=pltpu.CompilerParams(
                collective_id=0, has_side_effects=True, vmem_limit_bytes=48 * 2**20
            ),
        )(q, k, v, g)

    spec = P(("outer", "inner"), None, None)
    return jax.shard_map(
        step, mesh=mesh, in_specs=(spec,) * 4, out_specs=(spec,) * 3, check_vma=False
    )
```

```python
import functools

import jax
import jax.numpy as jnp
from jax import lax
from jax.experimental import pallas as pl
from jax.experimental.pallas import tpu as pltpu
from jax.sharding import PartitionSpec as P

MESH = pl.DeviceIdType.MESH
GROUPS = 4

PAIR, UP, ALONG, DOWN, BACK = range(5)


def nn(a, b):
    return lax.dot_general(a, b, (((1,), (0,)), ((), ())), preferred_element_type=jnp.float32)


def nt(a, b):
    return lax.dot_general(a, b, (((1,), (1,)), ((), ())), preferred_element_type=jnp.float32)


def tn(a, b):
    return lax.dot_general(a, b, (((0,), (0,)), ((), ())), preferred_element_type=jnp.float32)


def kernel(
    dims, scale,
    q_ref, k_ref, v_ref, g_ref, dq_ref, dk_ref, dv_ref,
    qt, kt, vt, gt, acc, res, own, pair, chip, got, plane, along, down, base, back, final,
    stage_in, load, send, recv,
):
    nz, nxy, groups = dims
    heads, tok, dim = qt.shape
    per = heads // groups
    half = per // 2
    rows = half * dim
    r = rows // nxy
    z = lax.axis_index("outer")
    inner = lax.axis_index("inner")
    xy, core = inner // 2, inner % 2

    def there(dz, dxy, dcore):
        return (lax.rem(z + dz, nz), lax.rem(xy + dxy, nxy) * 2 + lax.rem(core + dcore, 2))

    for i, src in enumerate((k_ref, v_ref, q_ref, g_ref)):
        pltpu.make_async_copy(src, stage_in.at[i], load.at[i]).start()

    partners = [there(0, 0, 1)]
    partners += [there(0, k, 0) for k in range(1, nxy)]
    partners += [there(k, 0, 0) for k in range(1, nz)]
    barrier = pltpu.get_barrier_semaphore()
    for who in partners:
        pl.semaphore_signal(barrier, inc=1, device_id=who, device_id_type=MESH)

    def remote(src, dst, stage, g, who):
        return pltpu.make_async_remote_copy(
            src_ref=src, dst_ref=dst, send_sem=send.at[stage, g], recv_sem=recv.at[stage, g],
            device_id=who, device_id_type=MESH,
        )

    def arrived(ref, stage, g):
        pltpu.make_async_copy(ref, ref, recv.at[stage, g]).wait()

    def left(ref, stage, g):
        pltpu.make_async_copy(ref, ref, send.at[stage, g]).wait()

    for i, (src, to) in enumerate(((k_ref, kt), (v_ref, vt), (q_ref, qt), (g_ref, gt))):
        pltpu.make_async_copy(src, stage_in.at[i], load.at[i]).wait()
        to[...] = jnp.swapaxes(stage_in[i], 0, 1)

    def states(g):
        for part in range(2):
            def one(j, _, part=part):
                h = g * per + part * half + j
                at = pl.ds(pl.multiple_of(j * dim, dim), dim)
                own[g, part, 0, at] = tn(kt[h], vt[h])
                own[g, part, 1, at] = tn(qt[h], gt[h])
                return 0
            lax.fori_loop(0, half, one, 0, unroll=min(2, half))

    def pair_start(g):
        remote(own.at[g, 1 - core], pair.at[g], PAIR, g, there(0, 0, 1)).start()

    def up_start(g):
        arrived(pair.at[g], PAIR, g)
        for s in range(2):
            total = own[g, core, s] + pair[g, s]
            chip[g, :, s] = total.reshape(nxy, r, dim)
        pltpu.make_async_copy(chip.at[g, xy], got.at[g, xy], recv.at[UP, g]).start()
        for k in range(1, nxy):
            who = lax.rem(xy + k, nxy)
            remote(chip.at[g, who], got.at[g, xy], UP, g, there(0, k, 0)).start()

    def along_start(g):
        arrived(got.at[g], UP, g)
        plane[g] = jnp.sum(got[g], axis=0)
        for k in range(1, nz):
            later = lax.rem(z + k, nz) > z
            remote(plane.at[g, jnp.where(later, 0, 1)], along.at[g, k - 1], ALONG, g, there(k, 0, 0)).start()

    def down_start(g):
        arrived(along.at[g], ALONG, g)
        before = jnp.zeros((r, dim), jnp.float32)
        after = jnp.zeros((r, dim), jnp.float32)
        for k in range(1, nz):
            value = along[g, k - 1]
            before = before + jnp.where(k <= z, value, 0.0)
            after = after + jnp.where(k > z, value, 0.0)
        for i in range(nxy):
            down[g, i, 0] = before
            before = before + got[g, i, 0]
        for i in reversed(range(nxy)):
            down[g, i, 1] = after
            after = after + got[g, i, 1]
        pltpu.make_async_copy(down.at[g, xy], base.at[g, xy], recv.at[DOWN, g]).start()
        for k in range(1, nxy):
            who = lax.rem(xy + k, nxy)
            remote(down.at[g, who], base.at[g, xy], DOWN, g, there(0, k, 0)).start()

    def back_start(g):
        arrived(base.at[g], DOWN, g)
        first = core == 0
        before = base[g, :, 0].reshape(rows, dim)
        after = base[g, :, 1].reshape(rows, dim)
        back[g, 0] = before + jnp.where(first, own[g, core, 0], 0.0)
        back[g, 1] = after + jnp.where(first, 0.0, own[g, core, 1])
        remote(back.at[g], final.at[g, 1], BACK, g, there(0, 0, 1)).start()
        final[g, 0, 0] = before + jnp.where(first, 0.0, pair[g, 0])
        final[g, 0, 1] = after + jnp.where(first, pair[g, 1], 0.0)

    def local(h, _):
        at = lax.broadcasted_iota(jnp.int32, (tok, tok), 0)
        to = lax.broadcasted_iota(jnp.int32, (tok, tok), 1)
        q, k, v, d = qt[h], kt[h], vt[h], gt[h]
        dprob = jnp.where(to <= at, nt(d, v), 0.0).astype(jnp.bfloat16)
        dprob_t = jnp.where(at <= to, nt(v, d), 0.0).astype(jnp.bfloat16)
        score_t = jnp.where(at <= to, nt(k, q), 0.0).astype(jnp.bfloat16)
        acc[0, h] = nn(dprob, k)
        acc[1, h] = nn(dprob_t, q)
        acc[2, h] = nn(score_t, d)
        return 0

    def finish(g, which):
        part = core if which == 0 else 1 - core

        def one(j, _):
            h = g * per + part * half + j
            at = pl.ds(pl.multiple_of(j * dim, dim), dim)
            before = final[g, which, 0, at].astype(jnp.bfloat16)
            after = final[g, which, 1, at].astype(jnp.bfloat16)
            res[0, h] = (scale * (acc[0, h] + nt(gt[h], before))).astype(jnp.bfloat16)
            res[1, h] = (scale * (acc[1, h] + nt(vt[h], after))).astype(jnp.bfloat16)
            res[2, h] = (scale * (acc[2, h] + nn(kt[h], after))).astype(jnp.bfloat16)
            return 0

        lax.fori_loop(0, half, one, 0, unroll=min(2, half))

    def local_group(g):
        lax.fori_loop(g * per, (g + 1) * per, local, 0, unroll=2)

    states(0)
    pl.semaphore_wait(barrier, len(partners))
    pair_start(0)
    for g in range(1, groups):
        states(g)
        pair_start(g)
        up_start(g - 1)
    up_start(groups - 1)
    for g in range(groups):
        local_group(g)
    for g in range(groups):
        along_start(g)
        if g >= 1:
            down_start(g - 1)
    down_start(groups - 1)
    for g in range(groups):
        back_start(g)
        finish(g, 0)
        arrived(final.at[g, 1], BACK, g)
        finish(g, 1)
    dq_ref[...] = jnp.swapaxes(res[0], 0, 1)
    dk_ref[...] = jnp.swapaxes(res[1], 0, 1)
    dv_ref[...] = jnp.swapaxes(res[2], 0, 1)

    for g in range(groups):
        left(pair.at[g], PAIR, g)
        left(chip.at[g, pl.ds(0, nxy - 1)], UP, g)
        left(along.at[g], ALONG, g)
        left(down.at[g, pl.ds(0, nxy - 1)], DOWN, g)
        left(back.at[g], BACK, g)


def keep(a, b, c, oa, ob, oc, sems):
    copies = [pltpu.make_async_copy(x, o, sems.at[i]) for i, (x, o) in enumerate(((a, oa), (b, ob), (c, oc)))]
    for copy in copies:
        copy.start()
    for copy in copies:
        copy.wait()


def solution(mesh):
    nz, nxy = mesh.shape["outer"], mesh.shape["inner"] // 2
    groups = GROUPS

    def step(q, k, v, g):
        tok, heads, dim = q.shape
        scale = (dim * tok * mesh.size) ** -0.5
        rows = heads // groups // 2 * dim
        r = rows // nxy
        f32, low = jnp.float32, jnp.bfloat16
        vmem = pl.BlockSpec(memory_space=pltpu.VMEM)
        grads = pl.pallas_call(
            functools.partial(kernel, (nz, nxy, groups), scale),
            out_shape=[jax.ShapeDtypeStruct((tok, heads, dim), low)] * 3,
            in_specs=[pl.BlockSpec(memory_space=pltpu.HBM)] * 4,
            out_specs=[vmem] * 3,
            scratch_shapes=[
                pltpu.VMEM((heads, tok, dim), low),
                pltpu.VMEM((heads, tok, dim), low),
                pltpu.VMEM((heads, tok, dim), low),
                pltpu.VMEM((heads, tok, dim), low),
                pltpu.VMEM((3, heads, tok, dim), f32),
                pltpu.VMEM((3, heads, tok, dim), low),
                pltpu.VMEM((groups, 2, 2, rows, dim), f32),
                pltpu.VMEM((groups, 2, rows, dim), f32),
                pltpu.VMEM((groups, nxy, 2, r, dim), f32),
                pltpu.VMEM((groups, nxy, 2, r, dim), f32),
                pltpu.VMEM((groups, 2, r, dim), f32),
                pltpu.VMEM((groups, nz - 1, r, dim), f32),
                pltpu.VMEM((groups, nxy, 2, r, dim), f32),
                pltpu.VMEM((groups, nxy, 2, r, dim), f32),
                pltpu.VMEM((groups, 2, rows, dim), f32),
                pltpu.VMEM((groups, 2, 2, rows, dim), f32),
                pltpu.VMEM((4, tok, heads, dim), low),
                pltpu.SemaphoreType.DMA((4,)),
                pltpu.SemaphoreType.DMA((5, groups)),
                pltpu.SemaphoreType.DMA((5, groups)),
            ],
            compiler_params=pltpu.CompilerParams(
                collective_id=0, has_side_effects=True, vmem_limit_bytes=54525952
            ),
        )(q, k, v, g)
        return pl.pallas_call(
            keep,
            out_shape=[jax.ShapeDtypeStruct((tok, heads, dim), low)] * 3,
            in_specs=[pl.BlockSpec(memory_space=pl.ANY)] * 3,
            out_specs=[pl.BlockSpec(memory_space=pl.ANY)] * 3,
            scratch_shapes=[pltpu.SemaphoreType.DMA((3,))],
            compiler_params=pltpu.CompilerParams(vmem_limit_bytes=2**20),
        )(*grads)

    spec = P(("outer", "inner"), None, None)
    return jax.shard_map(
        step, mesh=mesh, in_specs=(spec,) * 4, out_specs=(spec,) * 3, check_vma=False
    )
```

```python
import functools

import jax
import jax.numpy as jnp
from jax import lax
from jax.experimental import pallas as pl
from jax.experimental.pallas import tpu as pltpu
from jax.sharding import PartitionSpec as P

MESH = pl.DeviceIdType.MESH
SIZES = (8, 8)

PAIR, UP, DOWN, BACK = range(4)


def nn(a, b):
    return lax.dot_general(a, b, (((1,), (0,)), ((), ())), preferred_element_type=jnp.float32)


def nt(a, b):
    return lax.dot_general(a, b, (((1,), (1,)), ((), ())), preferred_element_type=jnp.float32)


def tn(a, b):
    return lax.dot_general(a, b, (((0,), (0,)), ((), ())), preferred_element_type=jnp.float32)


def spread(nxy):
    nx = max(n for n in range(1, nxy + 1) if n * n <= nxy and nxy % n == 0)
    ny = nxy // nx
    order = ((2, 2), (2, 1), (1, 2), (2, 3), (3, 2), (2, 0), (0, 2), (1, 1), (3, 3), (1, 3), (3, 1), (1, 0), (0, 1), (3, 0), (0, 3))
    if (nx, ny) != (4, 4):
        order = [(a, b) for a in range(nx) for b in range(ny) if a or b]
    return nx, ny, order


def unroll(count):
    return next(n for n in (4, 3, 2, 1) if count % n == 0)


def kernel(dims, scale, k_ref, v_ref, q_ref, g_ref, dq_ref, dk_ref, dv_ref, raw, low, acc, *rest):
    nz, nxy, sizes = dims
    count = len(sizes)
    load, send, recv, zsend, zrecv = rest[-5:]
    buffers = [rest[10 * i : 10 * i + 10] for i in range(count)]
    heads, tok, dim = acc.shape[1:]
    begins = [sum(sizes[:i]) for i in range(count)]
    z = lax.axis_index("outer")
    inner = lax.axis_index("inner")
    xy, core = inner // 2, inner % 2
    lead = jnp.where(z < nz // 2, 0, 1)

    def there(dz, dxy, dcore):
        return (lax.rem(z + dz, nz), lax.rem(xy + dxy, nxy) * 2 + lax.rem(core + dcore, 2))

    nx, ny, order = spread(nxy)
    x, y = xy // ny, xy % ny

    def across(a, b):
        if nx == ny:
            a, b = jnp.where(core == 0, a, b), jnp.where(core == 0, b, a)
        return lax.rem(x + a, nx) * ny + lax.rem(y + b, ny)

    def to_plane(src, dst, stage, n, s):
        for a, b in order:
            who = across(a, b)
            remote(src.at[s, who], dst.at[s, xy], stage, n, s, (z, who * 2 + core)).start()
        pltpu.make_async_copy(src.at[s, xy], dst.at[s, xy], recv.at[stage, n, s]).start()

    partners = [there(0, 0, 1)]
    partners += [there(0, k, 0) for k in range(1, nxy)]
    partners += [there(k, 0, 0) for k in range(1, nz)]
    barrier = pltpu.get_barrier_semaphore()
    for who in partners:
        pl.semaphore_signal(barrier, inc=1, device_id=who, device_id_type=MESH)

    inputs = (k_ref, v_ref, q_ref, g_ref)

    def fetch(i):
        pltpu.make_async_copy(inputs[i], raw.at[i], load.at[i]).start()

    @pl.when(lead == 0)
    def _():
        for i in (0, 1, 2, 3):
            fetch(i)

    @pl.when(lead == 1)
    def _():
        for i in (2, 3, 0, 1):
            fetch(i)

    def remote(src, dst, stage, n, s, who):
        return pltpu.make_async_remote_copy(
            src_ref=src, dst_ref=dst, send_sem=send.at[stage, n, s], recv_sem=recv.at[stage, n, s],
            device_id=who, device_id_type=MESH,
        )

    def arrived(ref, stage, n, s):
        pltpu.make_async_copy(ref, ref, recv.at[stage, n, s]).wait()

    def left(ref, stage, n, s):
        pltpu.make_async_copy(ref, ref, send.at[stage, n, s]).wait()

    def by_head(s, first, heads_now):
        for i in range(2):
            at = 2 * s + i
            if first == 0:
                pltpu.make_async_copy(raw.at[at], raw.at[at], load.at[at]).wait()
            some = pl.ds(first, heads_now)
            low[at, some] = jnp.swapaxes(raw[at, :, some], 0, 1)

    def states(n, s, part):
        own = buffers[n][0]
        half = sizes[n] // 2

        def one(j, _):
            h = begins[n] + part * half + j
            own[s, part, pl.ds(pl.multiple_of(j * dim, dim), dim)] = tn(low[2 * s, h], low[2 * s + 1, h])
            return 0

        lax.fori_loop(0, half, one, 0, unroll=unroll(half))

    def pair_start(n, s):
        own, pair = buffers[n][:2]
        states(n, s, 1 - core)
        if n == 0 and s is lead:
            pl.semaphore_wait(barrier, len(partners))
        remote(own.at[s, 1 - core], pair.at[s], PAIR, n, s, there(0, 0, 1)).start()
        states(n, s, core)

    def up_start(n, s):
        own, pair, chip, got = buffers[n][:4]
        arrived(pair.at[s], PAIR, n, s)
        chip[s] = (own[s, core] + pair[s]).reshape(chip.shape[1:])
        to_plane(chip, got, UP, n, s)

    def z_copy(n, s, j):
        plane, along = buffers[n][4:6]
        to = jnp.where(s == 0, z + 1 + j, z - 1 - j)
        return pltpu.make_async_remote_copy(
            src_ref=plane.at[s], dst_ref=along.at[s, j], send_sem=zsend.at[n, s, j], recv_sem=zrecv.at[n, s, j],
            device_id=(to, inner), device_id_type=MESH,
        )

    def z_targets(s):
        return jnp.where(s == 0, nz - 1 - z, z)

    def z_sources(s):
        return jnp.where(s == 0, z, nz - 1 - z)

    def along_start(n, s):
        got, plane = buffers[n][3:5]
        arrived(got.at[s], UP, n, s)
        plane[s] = jnp.sum(got[s], axis=0)
        targets = z_targets(s)

        def one(j, _):
            z_copy(n, s, targets - 1 - j).start()
            return 0

        lax.fori_loop(0, targets, one, 0)

    def down_start(n, s):
        _, _, _, got, plane, along, down, base = buffers[n][:8]

        def one(j, total):
            pltpu.make_async_copy(along.at[s, j], along.at[s, j], zrecv.at[n, s, j]).wait()
            return total + along[s, j]

        total = lax.fori_loop(0, z_sources(s), one, jnp.zeros(plane.shape[1:], jnp.float32))
        for i in range(nxy):
            at = jnp.where(s == 0, i, nxy - 1 - i)
            down[s, at] = total
            total = total + got[s, at]
        to_plane(down, base, DOWN, n, s)

    def back_start(n, s):
        own, pair, _, _, _, _, _, base, back, final = buffers[n]
        arrived(base.at[s], DOWN, n, s)
        second = core + s == 1
        sums = base[s].reshape(back.shape[1:])
        back[s] = sums + jnp.where(second, 0.0, own[s, core])
        remote(back.at[s], final.at[s, 1], BACK, n, s, there(0, 0, 1)).start()
        final[s, 0] = sums + jnp.where(second, pair[s], 0.0)

    def local(h, _):
        at = lax.broadcasted_iota(jnp.int32, (tok, tok), 0)
        to = lax.broadcasted_iota(jnp.int32, (tok, tok), 1)
        k, v, q, d = low[0, h], low[1, h], low[2, h], low[3, h]
        dprob = jnp.where(to <= at, nt(d, v), 0.0).astype(jnp.bfloat16)
        dprob_t = jnp.where(at <= to, nt(v, d), 0.0).astype(jnp.bfloat16)
        score_t = jnp.where(at <= to, nt(k, q), 0.0).astype(jnp.bfloat16)
        acc[0, h] = nn(dprob, k)
        acc[1, h] = nn(dprob_t, q)
        acc[2, h] = nn(score_t, d)
        return 0

    def finish(n, s, which):
        final = buffers[n][9]
        half = sizes[n] // 2
        part = core if which == 0 else 1 - core

        def place(j):
            return begins[n] + part * half + j, pl.ds(pl.multiple_of(j * dim, dim), dim)

        def query_part(j, _):
            h, at = place(j)
            state = final[0, which, at].astype(jnp.bfloat16)
            dq_ref[h] = (scale * (acc[0, h] + nt(low[3, h], state))).astype(jnp.bfloat16)
            return 0

        def key_value_part(j, _):
            h, at = place(j)
            state = final[1, which, at].astype(jnp.bfloat16)
            dk_ref[h] = (scale * (acc[1, h] + nt(low[1, h], state))).astype(jnp.bfloat16)
            dv_ref[h] = (scale * (acc[2, h] + nn(low[0, h], state))).astype(jnp.bfloat16)
            return 0

        @pl.when(s == 0)
        def _():
            lax.fori_loop(0, half, query_part, 0, unroll=unroll(half))

        @pl.when(s == 1)
        def _():
            lax.fori_loop(0, half, key_value_part, 0, unroll=unroll(half))

    def finish_other(n, s):
        arrived(buffers[n][9].at[s, 1], BACK, n, s)
        finish(n, s, 1)

    def drain(i):
        n, s = jobs[i]
        _, pair, chip, _, plane, _, down, _, _, _ = buffers[n]
        left(pair.at[s], PAIR, n, s)
        left(chip.at[s, pl.ds(0, nxy - 1)], UP, n, s)
        if i < last:
            left(down.at[s, pl.ds(0, nxy - 1)], DOWN, n, s)

        def one(j, _):
            pltpu.make_async_copy(plane.at[s], plane.at[s], zsend.at[n, s, j]).wait()
            return 0

        lax.fori_loop(0, z_targets(s), one, 0)

    other = 1 - lead
    jobs = [(n, lead) for n in range(count)] + [(n, other) for n in reversed(range(count))]
    last = len(jobs) - 1
    eight = heads // 2
    by_head(lead, 0, eight)
    pair_start(*jobs[0])
    by_head(lead, eight, eight)
    pair_start(*jobs[1])
    up_start(*jobs[0])
    by_head(other, 0, eight)
    by_head(other, eight, eight)
    for i in range(2, last + 1):
        pair_start(*jobs[i])
        up_start(*jobs[i - 1])
    up_start(*jobs[last])
    def local_part(i):
        begin, end = heads * i // last, heads * (i + 1) // last
        lax.fori_loop(begin, end, local, 0, unroll=unroll(end - begin))

    for i, job in enumerate(jobs):
        if i < last:
            local_part(i)
        along_start(*job)
        if i >= 1:
            down_start(*jobs[i - 1])
    down_start(*jobs[last])
    for i, job in enumerate(jobs):
        if i == last:
            for j in range(last + 1):
                drain(j)
        back_start(*job)
        if i >= 1:
            finish_other(*jobs[i - 1])
        finish(*job, 0)
    finish_other(*jobs[last])
    left(buffers[jobs[last][0]][6].at[jobs[last][1], pl.ds(0, nxy - 1)], DOWN, *jobs[last])
    for n, s in jobs:
        left(buffers[n][8].at[s], BACK, n, s)


def by_token(a, b, c, oa, ob, oc, turned, sems):
    copies = []
    for i, (x, o) in enumerate(((a, oa), (b, ob), (c, oc))):
        turned[i] = jnp.swapaxes(x[...], 0, 1)
        copies.append(pltpu.make_async_copy(turned.at[i], o, sems.at[i]))
        copies[-1].start()
    for copy in copies:
        copy.wait()


def solution(mesh):
    nz, nxy = mesh.shape["outer"], mesh.shape["inner"] // 2
    f32, bf16 = jnp.float32, jnp.bfloat16

    def step(q, k, v, g):
        tok, heads, dim = q.shape
        assert sum(SIZES) == heads
        scale = (dim * tok * mesh.size) ** -0.5
        scratch = [
            pltpu.VMEM((4, tok, heads, dim), bf16),
            pltpu.VMEM((4, heads, tok, dim), bf16),
            pltpu.VMEM((3, heads, tok, dim), f32),
        ]
        for size in SIZES:
            rows = size // 2 * dim
            r = rows // nxy
            scratch += [
                pltpu.VMEM((2, 2, rows, dim), f32),
                pltpu.VMEM((2, rows, dim), f32),
                pltpu.VMEM((2, nxy, r, dim), f32),
                pltpu.VMEM((2, nxy, r, dim), f32),
                pltpu.VMEM((2, r, dim), f32),
                pltpu.VMEM((2, nz - 1, r, dim), f32),
                pltpu.VMEM((2, nxy, r, dim), f32),
                pltpu.VMEM((2, nxy, r, dim), f32),
                pltpu.VMEM((2, rows, dim), f32),
                pltpu.VMEM((2, 2, rows, dim), f32),
            ]
        count = len(SIZES)
        scratch += [
            pltpu.SemaphoreType.DMA((4,)),
            pltpu.SemaphoreType.DMA((4, count, 2)),
            pltpu.SemaphoreType.DMA((4, count, 2)),
            pltpu.SemaphoreType.DMA((count, 2, nz - 1)),
            pltpu.SemaphoreType.DMA((count, 2, nz - 1)),
        ]
        vmem, hbm = pl.BlockSpec(memory_space=pltpu.VMEM), pl.BlockSpec(memory_space=pltpu.HBM)
        whole = pl.BlockSpec(memory_space=pl.ANY)
        grads = pl.pallas_call(
            functools.partial(kernel, (nz, nxy, SIZES), scale),
            out_shape=[jax.ShapeDtypeStruct((heads, tok, dim), bf16)] * 3,
            in_specs=[hbm] * 4,
            out_specs=[vmem] * 3,
            scratch_shapes=scratch,
            compiler_params=pltpu.CompilerParams(
                collective_id=0, has_side_effects=True, vmem_limit_bytes=52 * 2**20
            ),
        )(k, v, q, g)
        return pl.pallas_call(
            by_token,
            out_shape=[jax.ShapeDtypeStruct((tok, heads, dim), bf16)] * 3,
            in_specs=[vmem] * 3,
            out_specs=[whole] * 3,
            scratch_shapes=[pltpu.VMEM((3, tok, heads, dim), bf16), pltpu.SemaphoreType.DMA((3,))],
            compiler_params=pltpu.CompilerParams(vmem_limit_bytes=4 * 2**20),
        )(*grads)

    spec = P(("outer", "inner"), None, None)
    return jax.shard_map(
        step, mesh=mesh, in_specs=(spec,) * 4, out_specs=(spec,) * 3, check_vma=False
    )
```

```python
import functools

import jax
import jax.numpy as jnp
from jax import lax
from jax.experimental import pallas as pl
from jax.experimental.pallas import tpu as pltpu
from jax.sharding import PartitionSpec as P

MESH = pl.DeviceIdType.MESH
SIZES = (8, 8)
BANDS = (2, 2, 4)

PAIR, UP, DOWN, BACK = range(4)


def nn(a, b):
    return lax.dot_general(a, b, (((1,), (0,)), ((), ())), preferred_element_type=jnp.float32)


def nt(a, b):
    return lax.dot_general(a, b, (((1,), (1,)), ((), ())), preferred_element_type=jnp.float32)


def tn(a, b):
    return lax.dot_general(a, b, (((0,), (0,)), ((), ())), preferred_element_type=jnp.float32)


def spread(nxy):
    nx = max(n for n in range(1, nxy + 1) if n * n <= nxy and nxy % n == 0)
    ny = nxy // nx
    order = ((2, 2), (2, 1), (1, 2), (2, 3), (3, 2), (2, 0), (0, 2), (1, 1), (3, 3), (1, 3), (3, 1), (1, 0), (0, 1), (3, 0), (0, 3))
    if (nx, ny) != (4, 4):
        order = [(a, b) for a in range(nx) for b in range(ny) if a or b]
    return nx, ny, order


def unroll(count):
    return next(n for n in (4, 3, 2, 1) if count % n == 0)


def kernel(dims, scale, k_ref, v_ref, q_ref, g_ref, dq_ref, dk_ref, dv_ref, raw, low, acc, *rest):
    nz, nxy, sizes = dims
    count = len(sizes)
    load, send, recv, zsend, zrecv = rest[-5:]
    buffers = [rest[10 * i : 10 * i + 10] for i in range(count)]
    heads, tok, dim = acc.shape[1:]
    begins = [sum(sizes[:i]) for i in range(count)]
    z = lax.axis_index("outer")
    inner = lax.axis_index("inner")
    xy, core = inner // 2, inner % 2
    lead = jnp.where(z < nz // 2, 0, 1)

    def there(dz, dxy, dcore):
        return (lax.rem(z + dz, nz), lax.rem(xy + dxy, nxy) * 2 + lax.rem(core + dcore, 2))

    nx, ny, order = spread(nxy)
    x, y = xy // ny, xy % ny

    def across(a, b):
        if nx == ny:
            a, b = jnp.where(core == 0, a, b), jnp.where(core == 0, b, a)
        return lax.rem(x + a, nx) * ny + lax.rem(y + b, ny)

    def to_plane(src, dst, stage, n, s):
        for a, b in order:
            who = across(a, b)
            remote(src.at[s, who], dst.at[s, xy], stage, n, s, (z, who * 2 + core)).start()
        pltpu.make_async_copy(src.at[s, xy], dst.at[s, xy], recv.at[stage, n, s]).start()

    bands = BANDS if nz == 8 else (nz // 2, nz - nz // 2)
    edges = [sum(bands[:i]) for i in range(len(bands) + 1)]
    low_edge = sum(jnp.where(z >= edge, edge - under, 0) for under, edge in zip(edges, edges[1:-1]))
    high_edge = nz - sum(jnp.where(z < edge, above - edge, 0) for edge, above in zip(edges[1:-1], edges[2:]))

    barrier = pltpu.get_barrier_semaphore()

    def greet(who):
        pl.semaphore_signal(barrier, inc=1, device_id=who, device_id_type=MESH)

    def greet_planes(begin, end):
        def one(at, _):
            @pl.when(at != z)
            def _():
                greet((at, inner))
            return 0

        lax.fori_loop(begin, end, one, 0)

    greet(there(0, 0, 1))
    for a, b in order:
        greet((z, across(a, b) * 2 + core))
    greet_planes(low_edge, high_edge)

    def first_wait():
        pl.semaphore_wait(barrier, nxy + high_edge - 1)
        greet_planes(high_edge, nz)
        greet_planes(0, low_edge)

    def second_wait():
        @pl.when(high_edge < nz)
        def _():
            pl.semaphore_wait(barrier, nz - high_edge)

    inputs = (k_ref, v_ref, q_ref, g_ref)

    def fetch(i):
        pltpu.make_async_copy(inputs[i], raw.at[i], load.at[i]).start()

    @pl.when(lead == 0)
    def _():
        for i in (0, 1, 2, 3):
            fetch(i)

    @pl.when(lead == 1)
    def _():
        for i in (2, 3, 0, 1):
            fetch(i)

    def remote(src, dst, stage, n, s, who):
        return pltpu.make_async_remote_copy(
            src_ref=src, dst_ref=dst, send_sem=send.at[stage, n, s], recv_sem=recv.at[stage, n, s],
            device_id=who, device_id_type=MESH,
        )

    def arrived(ref, stage, n, s):
        pltpu.make_async_copy(ref, ref, recv.at[stage, n, s]).wait()

    def left(ref, stage, n, s):
        pltpu.make_async_copy(ref, ref, send.at[stage, n, s]).wait()

    def by_head(s, first, heads_now):
        for i in range(2):
            at = 2 * s + i
            if first == 0:
                pltpu.make_async_copy(raw.at[at], raw.at[at], load.at[at]).wait()
            some = pl.ds(first, heads_now)
            low[at, some] = jnp.swapaxes(raw[at, :, some], 0, 1)

    def states(n, s, part):
        own = buffers[n][0]
        half = sizes[n] // 2

        def one(j, _):
            h = begins[n] + part * half + j
            own[s, part, pl.ds(pl.multiple_of(j * dim, dim), dim)] = tn(low[2 * s, h], low[2 * s + 1, h])
            return 0

        lax.fori_loop(0, half, one, 0, unroll=unroll(half))

    def pair_start(n, s):
        own, pair = buffers[n][:2]
        states(n, s, 1 - core)
        if n == 0 and s is lead:
            first_wait()
        remote(own.at[s, 1 - core], pair.at[s], PAIR, n, s, there(0, 0, 1)).start()
        states(n, s, core)

    def up_start(n, s):
        own, pair, chip, got = buffers[n][:4]
        arrived(pair.at[s], PAIR, n, s)
        chip[s] = (own[s, core] + pair[s]).reshape(chip.shape[1:])
        to_plane(chip, got, UP, n, s)

    def z_copy(n, s, j):
        plane, along = buffers[n][4:6]
        to = jnp.where(s == 0, z + 1 + j, z - 1 - j)
        return pltpu.make_async_remote_copy(
            src_ref=plane.at[s], dst_ref=along.at[s, j], send_sem=zsend.at[n, s, j], recv_sem=zrecv.at[n, s, j],
            device_id=(to, inner), device_id_type=MESH,
        )

    def z_targets(s):
        return jnp.where(s == 0, nz - 1 - z, z)

    def z_sources(s):
        return jnp.where(s == 0, z, nz - 1 - z)

    def along_start(n, s):
        got, plane = buffers[n][3:5]
        arrived(got.at[s], UP, n, s)
        plane[s] = jnp.sum(got[s], axis=0)
        targets = z_targets(s)

        def one(j, _):
            z_copy(n, s, targets - 1 - j).start()
            return 0

        lax.fori_loop(0, targets, one, 0)

    def down_start(n, s):
        _, _, _, got, plane, along, down, base = buffers[n][:8]

        def one(j, total):
            pltpu.make_async_copy(along.at[s, j], along.at[s, j], zrecv.at[n, s, j]).wait()
            return total + along[s, j]

        total = lax.fori_loop(0, z_sources(s), one, jnp.zeros(plane.shape[1:], jnp.float32))
        for i in range(nxy):
            at = jnp.where(s == 0, i, nxy - 1 - i)
            down[s, at] = total
            total = total + got[s, at]
        to_plane(down, base, DOWN, n, s)

    def back_start(n, s):
        own, pair, _, _, _, _, _, base, back, final = buffers[n]
        arrived(base.at[s], DOWN, n, s)
        second = core + s == 1
        sums = base[s].reshape(back.shape[1:])
        back[s] = sums + jnp.where(second, 0.0, own[s, core])
        remote(back.at[s], final.at[s, 1], BACK, n, s, there(0, 0, 1)).start()
        final[s, 0] = sums + jnp.where(second, pair[s], 0.0)

    def local(h, _):
        at = lax.broadcasted_iota(jnp.int32, (tok, tok), 0)
        to = lax.broadcasted_iota(jnp.int32, (tok, tok), 1)
        k, v, q, d = low[0, h], low[1, h], low[2, h], low[3, h]
        dprob = jnp.where(to <= at, nt(d, v), 0.0).astype(jnp.bfloat16)
        dprob_t = jnp.where(at <= to, nt(v, d), 0.0).astype(jnp.bfloat16)
        score_t = jnp.where(at <= to, nt(k, q), 0.0).astype(jnp.bfloat16)
        acc[0, h] = nn(dprob, k)
        acc[1, h] = nn(dprob_t, q)
        acc[2, h] = nn(score_t, d)
        return 0

    def finish(n, s, which):
        final = buffers[n][9]
        half = sizes[n] // 2
        part = core if which == 0 else 1 - core

        def place(j):
            return begins[n] + part * half + j, pl.ds(pl.multiple_of(j * dim, dim), dim)

        def query_part(j, _):
            h, at = place(j)
            state = final[0, which, at].astype(jnp.bfloat16)
            dq_ref[h] = (scale * (acc[0, h] + nt(low[3, h], state))).astype(jnp.bfloat16)
            return 0

        def key_value_part(j, _):
            h, at = place(j)
            state = final[1, which, at].astype(jnp.bfloat16)
            dk_ref[h] = (scale * (acc[1, h] + nt(low[1, h], state))).astype(jnp.bfloat16)
            dv_ref[h] = (scale * (acc[2, h] + nn(low[0, h], state))).astype(jnp.bfloat16)
            return 0

        @pl.when(s == 0)
        def _():
            lax.fori_loop(0, half, query_part, 0, unroll=unroll(half))

        @pl.when(s == 1)
        def _():
            lax.fori_loop(0, half, key_value_part, 0, unroll=unroll(half))

    def finish_other(n, s):
        arrived(buffers[n][9].at[s, 1], BACK, n, s)
        finish(n, s, 1)

    def drain(i):
        n, s = jobs[i]
        _, pair, chip, _, plane, _, down, _, _, _ = buffers[n]
        left(pair.at[s], PAIR, n, s)
        left(chip.at[s, pl.ds(0, nxy - 1)], UP, n, s)
        if i < last:
            left(down.at[s, pl.ds(0, nxy - 1)], DOWN, n, s)

        def one(j, _):
            pltpu.make_async_copy(plane.at[s], plane.at[s], zsend.at[n, s, j]).wait()
            return 0

        lax.fori_loop(0, z_targets(s), one, 0)

    other = 1 - lead
    jobs = [(n, lead) for n in range(count)] + [(n, other) for n in reversed(range(count))]
    last = len(jobs) - 1
    eight = heads // 2
    by_head(lead, 0, eight)
    pair_start(*jobs[0])
    by_head(lead, eight, eight)
    pair_start(*jobs[1])
    up_start(*jobs[0])
    by_head(other, 0, eight)
    by_head(other, eight, eight)
    for i in range(2, last + 1):
        pair_start(*jobs[i])
        up_start(*jobs[i - 1])
    up_start(*jobs[last])
    def local_part(i):
        begin, end = heads * i // last, heads * (i + 1) // last
        lax.fori_loop(begin, end, local, 0, unroll=unroll(end - begin))

    for i, job in enumerate(jobs):
        if i < last:
            local_part(i)
        if i == 0:
            second_wait()
        along_start(*job)
        if i >= 1:
            down_start(*jobs[i - 1])
    down_start(*jobs[last])
    for i, job in enumerate(jobs):
        if i == last:
            for j in range(last + 1):
                drain(j)
        back_start(*job)
        if i >= 1:
            finish_other(*jobs[i - 1])
        finish(*job, 0)
    finish_other(*jobs[last])
    left(buffers[jobs[last][0]][6].at[jobs[last][1], pl.ds(0, nxy - 1)], DOWN, *jobs[last])
    for n, s in jobs:
        left(buffers[n][8].at[s], BACK, n, s)


def by_token(a, b, c, oa, ob, oc, turned, sems):
    copies = []
    for i, (x, o) in enumerate(((a, oa), (b, ob), (c, oc))):
        turned[i] = jnp.swapaxes(x[...], 0, 1)
        copies.append(pltpu.make_async_copy(turned.at[i], o, sems.at[i]))
        copies[-1].start()
    for copy in copies:
        copy.wait()


def solution(mesh):
    nz, nxy = mesh.shape["outer"], mesh.shape["inner"] // 2
    f32, bf16 = jnp.float32, jnp.bfloat16

    def step(q, k, v, g):
        tok, heads, dim = q.shape
        assert sum(SIZES) == heads
        scale = (dim * tok * mesh.size) ** -0.5
        scratch = [
            pltpu.VMEM((4, tok, heads, dim), bf16),
            pltpu.VMEM((4, heads, tok, dim), bf16),
            pltpu.VMEM((3, heads, tok, dim), f32),
        ]
        for size in SIZES:
            rows = size // 2 * dim
            r = rows // nxy
            scratch += [
                pltpu.VMEM((2, 2, rows, dim), f32),
                pltpu.VMEM((2, rows, dim), f32),
                pltpu.VMEM((2, nxy, r, dim), f32),
                pltpu.VMEM((2, nxy, r, dim), f32),
                pltpu.VMEM((2, r, dim), f32),
                pltpu.VMEM((2, nz - 1, r, dim), f32),
                pltpu.VMEM((2, nxy, r, dim), f32),
                pltpu.VMEM((2, nxy, r, dim), f32),
                pltpu.VMEM((2, rows, dim), f32),
                pltpu.VMEM((2, 2, rows, dim), f32),
            ]
        count = len(SIZES)
        scratch += [
            pltpu.SemaphoreType.DMA((4,)),
            pltpu.SemaphoreType.DMA((4, count, 2)),
            pltpu.SemaphoreType.DMA((4, count, 2)),
            pltpu.SemaphoreType.DMA((count, 2, nz - 1)),
            pltpu.SemaphoreType.DMA((count, 2, nz - 1)),
        ]
        vmem, hbm = pl.BlockSpec(memory_space=pltpu.VMEM), pl.BlockSpec(memory_space=pltpu.HBM)
        whole = pl.BlockSpec(memory_space=pl.ANY)
        grads = pl.pallas_call(
            functools.partial(kernel, (nz, nxy, SIZES), scale),
            out_shape=[jax.ShapeDtypeStruct((heads, tok, dim), bf16)] * 3,
            in_specs=[hbm] * 4,
            out_specs=[vmem] * 3,
            scratch_shapes=scratch,
            compiler_params=pltpu.CompilerParams(
                collective_id=0, has_side_effects=True, vmem_limit_bytes=52 * 2**20
            ),
        )(k, v, q, g)
        return pl.pallas_call(
            by_token,
            out_shape=[jax.ShapeDtypeStruct((tok, heads, dim), bf16)] * 3,
            in_specs=[vmem] * 3,
            out_specs=[whole] * 3,
            scratch_shapes=[pltpu.VMEM((3, tok, heads, dim), bf16), pltpu.SemaphoreType.DMA((3,))],
            compiler_params=pltpu.CompilerParams(vmem_limit_bytes=4 * 2**20),
        )(*grads)

    spec = P(("outer", "inner"), None, None)
    return jax.shard_map(
        step, mesh=mesh, in_specs=(spec,) * 4, out_specs=(spec,) * 3, check_vma=False
    )
```

```python
import functools

import jax
import jax.numpy as jnp
from jax import lax
from jax.experimental import pallas as pl
from jax.experimental.pallas import tpu as pltpu
from jax.sharding import PartitionSpec as P

MESH = pl.DeviceIdType.MESH
SIZES = (8, 8)
BANDS = (3, 5)

PAIR, UP, DOWN, BACK = range(4)


def nn(a, b):
    return lax.dot_general(a, b, (((1,), (0,)), ((), ())), preferred_element_type=jnp.float32)


def nt(a, b):
    return lax.dot_general(a, b, (((1,), (1,)), ((), ())), preferred_element_type=jnp.float32)


def tn(a, b):
    return lax.dot_general(a, b, (((0,), (0,)), ((), ())), preferred_element_type=jnp.float32)


def spread(nxy):
    nx = max(n for n in range(1, nxy + 1) if n * n <= nxy and nxy % n == 0)
    ny = nxy // nx
    order = ((2, 2), (2, 1), (1, 2), (2, 3), (3, 2), (2, 0), (0, 2), (1, 1), (3, 3), (1, 3), (3, 1), (1, 0), (0, 1), (3, 0), (0, 3))
    if (nx, ny) != (4, 4):
        order = [(a, b) for a in range(nx) for b in range(ny) if a or b]
    return nx, ny, order


def unroll(count):
    return next(n for n in (4, 3, 2, 1) if count % n == 0)


def kernel(dims, scale, k_ref, v_ref, q_ref, g_ref, dq_ref, dk_ref, dv_ref, raw, low, acc, *rest):
    nz, nxy, sizes = dims
    count = len(sizes)
    load, send, recv, zsend, zrecv = rest[-5:]
    buffers = [rest[10 * i : 10 * i + 10] for i in range(count)]
    heads, tok, dim = acc.shape[1:]
    begins = [sum(sizes[:i]) for i in range(count)]
    z = lax.axis_index("outer")
    inner = lax.axis_index("inner")
    xy, core = inner // 2, inner % 2
    lead = jnp.where(z < 3, 0, 1)

    def there(dz, dxy, dcore):
        return (lax.rem(z + dz, nz), lax.rem(xy + dxy, nxy) * 2 + lax.rem(core + dcore, 2))

    nx, ny, order = spread(nxy)
    x, y = xy // ny, xy % ny

    def across(a, b):
        if nx == ny:
            a, b = jnp.where(core == 0, a, b), jnp.where(core == 0, b, a)
        return lax.rem(x + a, nx) * ny + lax.rem(y + b, ny)

    def to_plane(src, dst, stage, n, s):
        for a, b in order:
            who = across(a, b)
            remote(src.at[s, who], dst.at[s, xy], stage, n, s, (z, who * 2 + core)).start()
        pltpu.make_async_copy(src.at[s, xy], dst.at[s, xy], recv.at[stage, n, s]).start()

    bands = BANDS if nz == 8 else (nz // 2, nz - nz // 2)
    edges = [sum(bands[:i]) for i in range(len(bands) + 1)]
    low_edge = sum(jnp.where(z >= edge, edge - under, 0) for under, edge in zip(edges, edges[1:-1]))
    high_edge = nz - sum(jnp.where(z < edge, above - edge, 0) for edge, above in zip(edges[1:-1], edges[2:]))

    barrier = pltpu.get_barrier_semaphore()

    def greet(who):
        pl.semaphore_signal(barrier, inc=1, device_id=who, device_id_type=MESH)

    def greet_planes(begin, end):
        def one(at, _):
            @pl.when(at != z)
            def _():
                greet((at, inner))
            return 0

        lax.fori_loop(begin, end, one, 0)

    greet(there(0, 0, 1))
    for a, b in order:
        greet((z, across(a, b) * 2 + core))
    greet_planes(low_edge, high_edge)

    def first_wait():
        pl.semaphore_wait(barrier, nxy + high_edge - 1)
        greet_planes(high_edge, nz)
        greet_planes(0, low_edge)

    def second_wait():
        @pl.when(high_edge < nz)
        def _():
            pl.semaphore_wait(barrier, nz - high_edge)

    inputs = (k_ref, v_ref, q_ref, g_ref)

    def fetch(i):
        pltpu.make_async_copy(inputs[i], raw.at[i], load.at[i]).start()

    @pl.when(lead == 0)
    def _():
        for i in (0, 1, 2, 3):
            fetch(i)

    @pl.when(lead == 1)
    def _():
        for i in (2, 3, 0, 1):
            fetch(i)

    def remote(src, dst, stage, n, s, who):
        return pltpu.make_async_remote_copy(
            src_ref=src, dst_ref=dst, send_sem=send.at[stage, n, s], recv_sem=recv.at[stage, n, s],
            device_id=who, device_id_type=MESH,
        )

    def arrived(ref, stage, n, s):
        pltpu.make_async_copy(ref, ref, recv.at[stage, n, s]).wait()

    def left(ref, stage, n, s):
        pltpu.make_async_copy(ref, ref, send.at[stage, n, s]).wait()

    def by_head(s, first, heads_now):
        for i in range(2):
            at = 2 * s + i
            if first == 0:
                pltpu.make_async_copy(raw.at[at], raw.at[at], load.at[at]).wait()
            some = pl.ds(first, heads_now)
            low[at, some] = jnp.swapaxes(raw[at, :, some], 0, 1)

    def states(n, s, part):
        own = buffers[n][0]
        half = sizes[n] // 2

        def one(j, _):
            h = begins[n] + part * half + j
            own[s, part, pl.ds(pl.multiple_of(j * dim, dim), dim)] = tn(low[2 * s, h], low[2 * s + 1, h])
            return 0

        lax.fori_loop(0, half, one, 0, unroll=unroll(half))

    def pair_start(n, s):
        own, pair = buffers[n][:2]
        states(n, s, 1 - core)
        if n == 0 and s is lead:
            first_wait()
        remote(own.at[s, 1 - core], pair.at[s], PAIR, n, s, there(0, 0, 1)).start()
        states(n, s, core)

    def up_start(n, s):
        own, pair, chip, got = buffers[n][:4]
        arrived(pair.at[s], PAIR, n, s)
        chip[s] = (own[s, core] + pair[s]).reshape(chip.shape[1:])
        to_plane(chip, got, UP, n, s)

    def z_copy(n, s, j):
        plane, along = buffers[n][4:6]
        to = jnp.where(s == 0, z + 1 + j, z - 1 - j)
        return pltpu.make_async_remote_copy(
            src_ref=plane.at[s], dst_ref=along.at[s, j], send_sem=zsend.at[n, s, j], recv_sem=zrecv.at[n, s, j],
            device_id=(to, inner), device_id_type=MESH,
        )

    def z_targets(s):
        return jnp.where(s == 0, nz - 1 - z, z)

    def z_sources(s):
        return jnp.where(s == 0, z, nz - 1 - z)

    def along_start(n, s):
        got, plane = buffers[n][3:5]
        arrived(got.at[s], UP, n, s)
        plane[s] = jnp.sum(got[s], axis=0)
        targets = z_targets(s)

        def one(j, _):
            z_copy(n, s, targets - 1 - j).start()
            return 0

        lax.fori_loop(0, targets, one, 0)

    def down_start(n, s):
        _, _, _, got, plane, along, down, base = buffers[n][:8]

        def one(j, total):
            pltpu.make_async_copy(along.at[s, j], along.at[s, j], zrecv.at[n, s, j]).wait()
            return total + along[s, j]

        total = lax.fori_loop(0, z_sources(s), one, jnp.zeros(plane.shape[1:], jnp.float32))
        for i in range(nxy):
            at = jnp.where(s == 0, i, nxy - 1 - i)
            down[s, at] = total
            total = total + got[s, at]
        to_plane(down, base, DOWN, n, s)

    def back_start(n, s):
        own, pair, _, _, _, _, _, base, back, final = buffers[n]
        arrived(base.at[s], DOWN, n, s)
        second = core + s == 1
        sums = base[s].reshape(back.shape[1:])
        back[s] = sums + jnp.where(second, 0.0, own[s, core])
        remote(back.at[s], final.at[s, 1], BACK, n, s, there(0, 0, 1)).start()
        final[s, 0] = sums + jnp.where(second, pair[s], 0.0)

    def local(h, _):
        at = lax.broadcasted_iota(jnp.int32, (tok, tok), 0)
        to = lax.broadcasted_iota(jnp.int32, (tok, tok), 1)
        k, v, q, d = low[0, h], low[1, h], low[2, h], low[3, h]
        dprob = jnp.where(to <= at, nt(d, v), 0.0).astype(jnp.bfloat16)
        dprob_t = jnp.where(at <= to, nt(v, d), 0.0).astype(jnp.bfloat16)
        score_t = jnp.where(at <= to, nt(k, q), 0.0).astype(jnp.bfloat16)
        acc[0, h] = nn(dprob, k)
        acc[1, h] = nn(dprob_t, q)
        acc[2, h] = nn(score_t, d)
        return 0

    def finish(n, s, which):
        final = buffers[n][9]
        half = sizes[n] // 2
        part = core if which == 0 else 1 - core

        def place(j):
            return begins[n] + part * half + j, pl.ds(pl.multiple_of(j * dim, dim), dim)

        def query_part(j, _):
            h, at = place(j)
            state = final[0, which, at].astype(jnp.bfloat16)
            dq_ref[h] = (scale * (acc[0, h] + nt(low[3, h], state))).astype(jnp.bfloat16)
            return 0

        def key_value_part(j, _):
            h, at = place(j)
            state = final[1, which, at].astype(jnp.bfloat16)
            dk_ref[h] = (scale * (acc[1, h] + nt(low[1, h], state))).astype(jnp.bfloat16)
            dv_ref[h] = (scale * (acc[2, h] + nn(low[0, h], state))).astype(jnp.bfloat16)
            return 0

        @pl.when(s == 0)
        def _():
            lax.fori_loop(0, half, query_part, 0, unroll=unroll(half))

        @pl.when(s == 1)
        def _():
            lax.fori_loop(0, half, key_value_part, 0, unroll=unroll(half))

    def finish_other(n, s):
        arrived(buffers[n][9].at[s, 1], BACK, n, s)
        finish(n, s, 1)

    def drain(i):
        n, s = jobs[i]
        _, pair, chip, _, plane, _, down, _, _, _ = buffers[n]
        left(pair.at[s], PAIR, n, s)
        left(chip.at[s, pl.ds(0, nxy - 1)], UP, n, s)
        if i < last:
            left(down.at[s, pl.ds(0, nxy - 1)], DOWN, n, s)

        def one(j, _):
            pltpu.make_async_copy(plane.at[s], plane.at[s], zsend.at[n, s, j]).wait()
            return 0

        lax.fori_loop(0, z_targets(s), one, 0)

    other = 1 - lead
    jobs = [(n, lead) for n in range(count)] + [(n, other) for n in reversed(range(count))]
    last = len(jobs) - 1
    eight = heads // 2
    by_head(lead, 0, eight)
    pair_start(*jobs[0])
    by_head(lead, eight, eight)
    pair_start(*jobs[1])
    up_start(*jobs[0])
    by_head(other, 0, eight)
    by_head(other, eight, eight)
    for i in range(2, last + 1):
        pair_start(*jobs[i])
        up_start(*jobs[i - 1])
    up_start(*jobs[last])
    def local_part(i):
        begin, end = heads * i // last, heads * (i + 1) // last
        lax.fori_loop(begin, end, local, 0, unroll=unroll(end - begin))

    for i, job in enumerate(jobs):
        if i < last:
            local_part(i)
        if i == 0:
            second_wait()
        along_start(*job)
        if i >= 1:
            down_start(*jobs[i - 1])
    down_start(*jobs[last])
    for i, job in enumerate(jobs):
        if i == last:
            for j in range(last + 1):
                drain(j)
        back_start(*job)
        if i >= 1:
            finish_other(*jobs[i - 1])
        finish(*job, 0)
    finish_other(*jobs[last])
    left(buffers[jobs[last][0]][6].at[jobs[last][1], pl.ds(0, nxy - 1)], DOWN, *jobs[last])
    for n, s in jobs:
        left(buffers[n][8].at[s], BACK, n, s)


def by_token(a, b, c, oa, ob, oc, turned, sems):
    copies = []
    for i, (x, o) in enumerate(((a, oa), (b, ob), (c, oc))):
        turned[i] = jnp.swapaxes(x[...], 0, 1)
        copies.append(pltpu.make_async_copy(turned.at[i], o, sems.at[i]))
        copies[-1].start()
    for copy in copies:
        copy.wait()


def solution(mesh):
    nz, nxy = mesh.shape["outer"], mesh.shape["inner"] // 2
    f32, bf16 = jnp.float32, jnp.bfloat16

    def step(q, k, v, g):
        tok, heads, dim = q.shape
        assert sum(SIZES) == heads
        scale = (dim * tok * mesh.size) ** -0.5
        scratch = [
            pltpu.VMEM((4, tok, heads, dim), bf16),
            pltpu.VMEM((4, heads, tok, dim), bf16),
            pltpu.VMEM((3, heads, tok, dim), f32),
        ]
        for size in SIZES:
            rows = size // 2 * dim
            r = rows // nxy
            scratch += [
                pltpu.VMEM((2, 2, rows, dim), f32),
                pltpu.VMEM((2, rows, dim), f32),
                pltpu.VMEM((2, nxy, r, dim), f32),
                pltpu.VMEM((2, nxy, r, dim), f32),
                pltpu.VMEM((2, r, dim), f32),
                pltpu.VMEM((2, nz - 1, r, dim), f32),
                pltpu.VMEM((2, nxy, r, dim), f32),
                pltpu.VMEM((2, nxy, r, dim), f32),
                pltpu.VMEM((2, rows, dim), f32),
                pltpu.VMEM((2, 2, rows, dim), f32),
            ]
        count = len(SIZES)
        scratch += [
            pltpu.SemaphoreType.DMA((4,)),
            pltpu.SemaphoreType.DMA((4, count, 2)),
            pltpu.SemaphoreType.DMA((4, count, 2)),
            pltpu.SemaphoreType.DMA((count, 2, nz - 1)),
            pltpu.SemaphoreType.DMA((count, 2, nz - 1)),
        ]
        vmem, hbm = pl.BlockSpec(memory_space=pltpu.VMEM), pl.BlockSpec(memory_space=pltpu.HBM)
        whole = pl.BlockSpec(memory_space=pl.ANY)
        grads = pl.pallas_call(
            functools.partial(kernel, (nz, nxy, SIZES), scale),
            out_shape=[jax.ShapeDtypeStruct((heads, tok, dim), bf16)] * 3,
            in_specs=[hbm] * 4,
            out_specs=[vmem] * 3,
            scratch_shapes=scratch,
            compiler_params=pltpu.CompilerParams(
                collective_id=0, has_side_effects=True, vmem_limit_bytes=52 * 2**20
            ),
        )(k, v, q, g)
        return pl.pallas_call(
            by_token,
            out_shape=[jax.ShapeDtypeStruct((tok, heads, dim), bf16)] * 3,
            in_specs=[vmem] * 3,
            out_specs=[whole] * 3,
            scratch_shapes=[pltpu.VMEM((3, tok, heads, dim), bf16), pltpu.SemaphoreType.DMA((3,))],
            compiler_params=pltpu.CompilerParams(vmem_limit_bytes=4 * 2**20),
        )(*grads)

    spec = P(("outer", "inner"), None, None)
    return jax.shard_map(
        step, mesh=mesh, in_specs=(spec,) * 4, out_specs=(spec,) * 3, check_vma=False
    )
```

```python
import functools

import jax
import jax.numpy as jnp
from jax import lax
from jax.experimental import pallas as pl
from jax.experimental.pallas import tpu as pltpu
from jax.sharding import PartitionSpec as P

MESH = pl.DeviceIdType.MESH
SIZES = (8, 8)
BANDS = (3, 5)

PAIR, UP, DOWN, BACK = range(4)


def nn(a, b):
    return lax.dot_general(a, b, (((1,), (0,)), ((), ())), preferred_element_type=jnp.float32)


def nt(a, b):
    return lax.dot_general(a, b, (((1,), (1,)), ((), ())), preferred_element_type=jnp.float32)


def tn(a, b):
    return lax.dot_general(a, b, (((0,), (0,)), ((), ())), preferred_element_type=jnp.float32)


def spread(nxy):
    nx = max(n for n in range(1, nxy + 1) if n * n <= nxy and nxy % n == 0)
    ny = nxy // nx
    order = ((2, 2), (2, 1), (1, 2), (2, 3), (3, 2), (2, 0), (0, 2), (1, 1), (3, 3), (1, 3), (3, 1), (1, 0), (0, 1), (3, 0), (0, 3))
    if (nx, ny) != (4, 4):
        order = [(a, b) for a in range(nx) for b in range(ny) if a or b]
    return nx, ny, order


def unroll(count):
    return next(n for n in (4, 3, 2, 1) if count % n == 0)


def kernel(dims, scale, k_ref, v_ref, q_ref, g_ref, dq_ref, dk_ref, dv_ref, raw, low, acc, *rest):
    nz, nxy, sizes = dims
    count = len(sizes)
    load, send, recv, zsend, zrecv = rest[-5:]
    buffers = [rest[10 * i : 10 * i + 10] for i in range(count)]
    heads, tok, dim = acc.shape[1:]
    begins = [sum(sizes[:i]) for i in range(count)]
    z = lax.axis_index("outer")
    inner = lax.axis_index("inner")
    xy, core = inner // 2, inner % 2
    lead = jnp.where(z < 3, 0, 1)

    def there(dz, dxy, dcore):
        return (lax.rem(z + dz, nz), lax.rem(xy + dxy, nxy) * 2 + lax.rem(core + dcore, 2))

    nx, ny, order = spread(nxy)
    x, y = xy // ny, xy % ny

    def across(a, b):
        if nx == ny:
            a, b = jnp.where(core == 0, a, b), jnp.where(core == 0, b, a)
        return lax.rem(x + a, nx) * ny + lax.rem(y + b, ny)

    def to_plane(src, dst, stage, n, s):
        for a, b in order:
            who = across(a, b)
            remote(src.at[s, who], dst.at[s, xy], stage, n, s, (z, who * 2 + core)).start()
        pltpu.make_async_copy(src.at[s, xy], dst.at[s, xy], recv.at[stage, n, s]).start()

    bands = BANDS if nz == 8 else (nz // 2, nz - nz // 2)
    edges = [sum(bands[:i]) for i in range(len(bands) + 1)]
    low_edge = sum(jnp.where(z >= edge, edge - under, 0) for under, edge in zip(edges, edges[1:-1]))
    high_edge = nz - sum(jnp.where(z < edge, above - edge, 0) for edge, above in zip(edges[1:-1], edges[2:]))

    barrier = pltpu.get_barrier_semaphore()

    def greet(who):
        pl.semaphore_signal(barrier, inc=1, device_id=who, device_id_type=MESH)

    def greet_planes(begin, end):
        def one(at, _):
            @pl.when(at != z)
            def _():
                greet((at, inner))
            return 0

        lax.fori_loop(begin, end, one, 0)

    greet(there(0, 0, 1))
    for a, b in order:
        greet((z, across(a, b) * 2 + core))
    greet_planes(low_edge, high_edge)

    def first_wait():
        pl.semaphore_wait(barrier, nxy + high_edge - 1)
        greet_planes(high_edge, nz)
        greet_planes(0, low_edge)

    def second_wait():
        @pl.when(high_edge < nz)
        def _():
            pl.semaphore_wait(barrier, nz - high_edge)

    inputs = (k_ref, v_ref, q_ref, g_ref)

    def fetch(i):
        pltpu.make_async_copy(inputs[i], raw.at[i], load.at[i]).start()

    @pl.when(lead == 0)
    def _():
        for i in (0, 1, 2, 3):
            fetch(i)

    @pl.when(lead == 1)
    def _():
        for i in (2, 3, 0, 1):
            fetch(i)

    def remote(src, dst, stage, n, s, who):
        return pltpu.make_async_remote_copy(
            src_ref=src, dst_ref=dst, send_sem=send.at[stage, n, s], recv_sem=recv.at[stage, n, s],
            device_id=who, device_id_type=MESH,
        )

    def arrived(ref, stage, n, s):
        pltpu.make_async_copy(ref, ref, recv.at[stage, n, s]).wait()

    def left(ref, stage, n, s):
        pltpu.make_async_copy(ref, ref, send.at[stage, n, s]).wait()

    def by_head(s, first, heads_now):
        for i in range(2):
            at = 2 * s + i
            if first == 0:
                pltpu.make_async_copy(raw.at[at], raw.at[at], load.at[at]).wait()
            some = pl.ds(first, heads_now)
            low[at, some] = jnp.swapaxes(raw[at, :, some], 0, 1)

    def states(n, s, part):
        own = buffers[n][0]
        half = sizes[n] // 2

        def one(j, _):
            h = begins[n] + part * half + j
            own[s, part, pl.ds(pl.multiple_of(j * dim, dim), dim)] = tn(low[2 * s, h], low[2 * s + 1, h])
            return 0

        lax.fori_loop(0, half, one, 0, unroll=unroll(half))

    def pair_start(n, s):
        own, pair = buffers[n][:2]
        states(n, s, 1 - core)
        if n == 0 and s is lead:
            first_wait()
        remote(own.at[s, 1 - core], pair.at[s], PAIR, n, s, there(0, 0, 1)).start()
        states(n, s, core)

    def up_start(n, s):
        own, pair, chip, got = buffers[n][:4]
        arrived(pair.at[s], PAIR, n, s)
        chip[s] = (own[s, core] + pair[s]).reshape(chip.shape[1:])
        to_plane(chip, got, UP, n, s)

    def z_copy(n, s, j):
        plane, along = buffers[n][4:6]
        to = jnp.where(s == 0, z + 1 + j, z - 1 - j)
        return pltpu.make_async_remote_copy(
            src_ref=plane.at[s], dst_ref=along.at[s, j], send_sem=zsend.at[n, s, j], recv_sem=zrecv.at[n, s, j],
            device_id=(to, inner), device_id_type=MESH,
        )

    def z_targets(s):
        return jnp.where(s == 0, nz - 1 - z, z)

    def z_sources(s):
        return jnp.where(s == 0, z, nz - 1 - z)

    def along_start(n, s):
        got, plane = buffers[n][3:5]
        arrived(got.at[s], UP, n, s)
        plane[s] = jnp.sum(got[s], axis=0)
        targets = z_targets(s)

        def one(j, _):
            z_copy(n, s, targets - 1 - j).start()
            return 0

        lax.fori_loop(0, targets, one, 0)

    def down_start(n, s):
        _, _, _, got, plane, along, down, base = buffers[n][:8]

        def one(j, total):
            pltpu.make_async_copy(along.at[s, j], along.at[s, j], zrecv.at[n, s, j]).wait()
            return total + along[s, j]

        total = lax.fori_loop(0, z_sources(s), one, jnp.zeros(plane.shape[1:], jnp.float32))
        for i in range(nxy):
            at = jnp.where(s == 0, i, nxy - 1 - i)
            down[s, at] = total
            total = total + got[s, at]
        to_plane(down, base, DOWN, n, s)

    def back_start(n, s):
        own, pair, _, _, _, _, _, base, back, final = buffers[n]
        arrived(base.at[s], DOWN, n, s)
        second = core + s == 1
        sums = base[s].reshape(back.shape[1:])
        back[s] = sums + jnp.where(second, 0.0, own[s, core])
        remote(back.at[s], final.at[s, 1], BACK, n, s, there(0, 0, 1)).start()
        final[s, 0] = sums + jnp.where(second, pair[s], 0.0)

    def local(h, _):
        at = lax.broadcasted_iota(jnp.int32, (tok, tok), 0)
        to = lax.broadcasted_iota(jnp.int32, (tok, tok), 1)
        k, v, q, d = low[0, h], low[1, h], low[2, h], low[3, h]
        dprob = jnp.where(to <= at, nt(d, v), 0.0).astype(jnp.bfloat16)
        dprob_t = jnp.where(at <= to, nt(v, d), 0.0).astype(jnp.bfloat16)
        score_t = jnp.where(at <= to, nt(k, q), 0.0).astype(jnp.bfloat16)
        acc[0, h] = nn(dprob, k)
        acc[1, h] = nn(dprob_t, q)
        acc[2, h] = nn(score_t, d)
        return 0

    def finish(n, s, which):
        final = buffers[n][9]
        half = sizes[n] // 2
        part = core if which == 0 else 1 - core

        def place(j):
            return begins[n] + part * half + j, pl.ds(pl.multiple_of(j * dim, dim), dim)

        def query_part(j, _):
            h, at = place(j)
            state = final[0, which, at].astype(jnp.bfloat16)
            dq_ref[h] = (scale * (acc[0, h] + nt(low[3, h], state))).astype(jnp.bfloat16)
            return 0

        def key_value_part(j, _):
            h, at = place(j)
            state = final[1, which, at].astype(jnp.bfloat16)
            dk_ref[h] = (scale * (acc[1, h] + nt(low[1, h], state))).astype(jnp.bfloat16)
            dv_ref[h] = (scale * (acc[2, h] + nn(low[0, h], state))).astype(jnp.bfloat16)
            return 0

        @pl.when(s == 0)
        def _():
            lax.fori_loop(0, half, query_part, 0, unroll=unroll(half))

        @pl.when(s == 1)
        def _():
            lax.fori_loop(0, half, key_value_part, 0, unroll=unroll(half))

    def finish_other(n, s):
        arrived(buffers[n][9].at[s, 1], BACK, n, s)
        finish(n, s, 1)

    def drain(i):
        n, s = jobs[i]
        _, pair, chip, _, plane, _, down, _, _, _ = buffers[n]
        left(pair.at[s], PAIR, n, s)
        left(chip.at[s, pl.ds(0, nxy - 1)], UP, n, s)
        if i < last:
            left(down.at[s, pl.ds(0, nxy - 1)], DOWN, n, s)

        def one(j, _):
            pltpu.make_async_copy(plane.at[s], plane.at[s], zsend.at[n, s, j]).wait()
            return 0

        lax.fori_loop(0, z_targets(s), one, 0)

    other = 1 - lead
    jobs = [(n, lead) for n in range(count)] + [(n, other) for n in reversed(range(count))]
    last = len(jobs) - 1
    eight = heads // 2
    by_head(lead, 0, eight)
    pair_start(*jobs[0])
    by_head(lead, eight, eight)
    pair_start(*jobs[1])
    up_start(*jobs[0])
    by_head(other, 0, eight)
    by_head(other, eight, eight)
    for i in range(2, last + 1):
        pair_start(*jobs[i])
        up_start(*jobs[i - 1])
    up_start(*jobs[last])
    def local_part(i):
        begin, end = heads * i // last, heads * (i + 1) // last
        lax.fori_loop(begin, end, local, 0, unroll=unroll(end - begin))

    for i, job in enumerate(jobs):
        if i < last:
            local_part(i)
        if i == 0:
            second_wait()
        along_start(*job)
        if i >= 1:
            down_start(*jobs[i - 1])
    down_start(*jobs[last])
    for i, job in enumerate(jobs):
        if i == last:
            for j in range(last + 1):
                drain(j)
        back_start(*job)
        if i >= 1:
            finish_other(*jobs[i - 1])
        finish(*job, 0)
    finish_other(*jobs[last])
    left(buffers[jobs[last][0]][6].at[jobs[last][1], pl.ds(0, nxy - 1)], DOWN, *jobs[last])
    for n, s in jobs:
        left(buffers[n][8].at[s], BACK, n, s)


def by_token(a, b, c, oa, ob, oc, turned, sems):
    parts = sems.shape[1]
    rows = a.shape[1] // parts
    copies = []
    for i, (x, o) in enumerate(((a, oa), (b, ob), (c, oc))):
        for j in range(parts):
            some = pl.ds(j * rows, rows)
            turned[i, some] = jnp.swapaxes(x[:, some], 0, 1)
            copies.append(pltpu.make_async_copy(turned.at[i, some], o.at[some], sems.at[i, j]))
            copies[-1].start()
    for copy in copies:
        copy.wait()


def solution(mesh):
    nz, nxy = mesh.shape["outer"], mesh.shape["inner"] // 2
    f32, bf16 = jnp.float32, jnp.bfloat16

    def step(q, k, v, g):
        tok, heads, dim = q.shape
        assert sum(SIZES) == heads
        scale = (dim * tok * mesh.size) ** -0.5
        scratch = [
            pltpu.VMEM((4, tok, heads, dim), bf16),
            pltpu.VMEM((4, heads, tok, dim), bf16),
            pltpu.VMEM((3, heads, tok, dim), f32),
        ]
        for size in SIZES:
            rows = size // 2 * dim
            r = rows // nxy
            scratch += [
                pltpu.VMEM((2, 2, rows, dim), f32),
                pltpu.VMEM((2, rows, dim), f32),
                pltpu.VMEM((2, nxy, r, dim), f32),
                pltpu.VMEM((2, nxy, r, dim), f32),
                pltpu.VMEM((2, r, dim), f32),
                pltpu.VMEM((2, nz - 1, r, dim), f32),
                pltpu.VMEM((2, nxy, r, dim), f32),
                pltpu.VMEM((2, nxy, r, dim), f32),
                pltpu.VMEM((2, rows, dim), f32),
                pltpu.VMEM((2, 2, rows, dim), f32),
            ]
        count = len(SIZES)
        scratch += [
            pltpu.SemaphoreType.DMA((4,)),
            pltpu.SemaphoreType.DMA((4, count, 2)),
            pltpu.SemaphoreType.DMA((4, count, 2)),
            pltpu.SemaphoreType.DMA((count, 2, nz - 1)),
            pltpu.SemaphoreType.DMA((count, 2, nz - 1)),
        ]
        vmem, hbm = pl.BlockSpec(memory_space=pltpu.VMEM), pl.BlockSpec(memory_space=pltpu.HBM)
        whole = pl.BlockSpec(memory_space=pl.ANY)
        grads = pl.pallas_call(
            functools.partial(kernel, (nz, nxy, SIZES), scale),
            out_shape=[jax.ShapeDtypeStruct((heads, tok, dim), bf16)] * 3,
            in_specs=[hbm] * 4,
            out_specs=[vmem] * 3,
            scratch_shapes=scratch,
            compiler_params=pltpu.CompilerParams(
                collective_id=0, has_side_effects=True, vmem_limit_bytes=52 * 2**20
            ),
        )(k, v, q, g)
        return pl.pallas_call(
            by_token,
            out_shape=[jax.ShapeDtypeStruct((tok, heads, dim), bf16)] * 3,
            in_specs=[vmem] * 3,
            out_specs=[whole] * 3,
            scratch_shapes=[pltpu.VMEM((3, tok, heads, dim), bf16), pltpu.SemaphoreType.DMA((3, 2))],
            compiler_params=pltpu.CompilerParams(vmem_limit_bytes=4 * 2**20),
        )(*grads)

    spec = P(("outer", "inner"), None, None)
    return jax.shard_map(
        step, mesh=mesh, in_specs=(spec,) * 4, out_specs=(spec,) * 3, check_vma=False
    )
```
